32 devices in a mesh: grp: 2 (over x), ang: 16 (over z, y, core).
Axes of the slice: x: 2, y: 2, z: 4, core: 2. Of those that a mesh axis runs over, the one named last changes fastest.
Arguments:
- projections: bfloat16 [64, 16, 16, 2048], P(('grp', 'ang')), parts along dimension 0, may hold values from -6 to 6
- cotangent: bfloat16 [64, 16, 16, 2048], P('grp', 'ang'), parts along dimension 0, may hold values from -6 to 6
- row_taps: bfloat16 [16, 65], replicated, may hold values from -0.75 to 0.75
- channel_mix: float32 [16, 16], replicated, may hold values from -1.5 to 1.5
- angle_taps: float32 [3, 16, 9], replicated, may hold values from -2 to 2
- angle_order: int32 [64], P('grp'), parts along dimension 0, may hold values from 0 to 31, each once
- dilations: int32 [3], replicated, may hold values from 1 to 7, as said below
Outputs:
- filtered: bfloat16 [64, 16, 16, 2048], P('grp', 'ang'), parts along dimension 0
- grad_input: bfloat16 [64, 16, 16, 2048], P(('grp', 'ang')), parts along dimension 0
- grad_row_taps: float32 [32, 65], P('grp'), parts along dimension 0
- grad_channel_mix: float32 [32, 16], P('grp'), parts along dimension 0
- grad_angle_taps: float32 [6, 16, 9], P('grp'), parts along dimension 0
The draws below stay inside these ranges and needn't reach their ends.
There are 2 independent parts, one for each index of `grp`. The reference program is written for one: setup_inputs(seed, part) draws one part's arguments, and reference() takes and returns one part's arrays. A program takes and returns all parts, laid end to end along the dimension named above; an argument that names none is the same for every part. Nothing has to cross between parts.
Inputs may be any that keep to these rules, and one draw needn't show every extreme that they name: `dilations`: each layer's dilation; some layer has exactly 7. `angle_order`: a permutation of the angle positions.
All inputs are finite; a program needn't handle non-finite values.
Results may differ from the reference program's by a relative error of at most 0.0071.
Values may be sent and summed in bfloat16 or wider, within the bound.
A program may use at most 128 MiB of HBM per device.

```python
import math
import jax
import jax.numpy as jnp
from jax import lax

CHANNELS = 16
COLUMNS = 2048
ROW_TAPS = 65
ANGLE_TAPS = 9
LAYERS = 3
ANGLES = 32
DET_ROWS = 16
MAX_DILATION = 7


def draw_dilations(key, part):
    folded = jax.random.fold_in(key, 17)
    first_key, second_key = jax.random.split(folded)
    values = jax.random.randint(first_key, (LAYERS,), 1, MAX_DILATION + 1)
    position = jax.random.randint(second_key, (), 0, LAYERS)
    values = values.at[position].set(MAX_DILATION)
    return values.astype(jnp.int32)


def levels(stream_key, shape, cuts, smallest, largest):
    def one(axis_at, shards_of):
        heights = jax.random.uniform(jax.random.fold_in(jax.random.fold_in(stream_key, 6), axis_at), (shards_of,), jnp.float32, smallest / len(cuts), largest / len(cuts))
        return jnp.repeat(jnp.exp(heights), shape[axis_at] // shards_of).reshape((-1,) + (1,) * (len(shape) - axis_at - 1))

    gain = one(*cuts[0])
    for cut in cuts[1:]:
        gain = gain * one(*cut)
    return gain


def gaussian(own_key, extent, width, limit, cuts=(), dtype=jnp.bfloat16):
    values = width * jax.random.normal(own_key, extent, jnp.float32)
    if cuts:
        values = values * levels(own_key, extent, cuts, -0.22, 0.18)
    return jnp.clip(values, -limit, limit).astype(dtype)


def setup_inputs(seed: int = 0, part: int = 0) -> dict:
    key_of = jax.random.split(jax.random.key(seed), 8)
    own_keys = jax.random.split(jax.random.fold_in(key_of[7], part), 8)
    projections = gaussian(own_keys[0], (ANGLES, DET_ROWS, CHANNELS, COLUMNS), 1.0, 6.0, ((0, 16),))
    cotangent = gaussian(own_keys[1], (ANGLES, DET_ROWS, CHANNELS, COLUMNS), 1.0, 6.0, ((1, 16),))
    row_taps = gaussian(key_of[2], (CHANNELS, ROW_TAPS), ROW_TAPS ** -0.5, 0.75)
    channel_mix = gaussian(key_of[3], (CHANNELS, CHANNELS), CHANNELS ** -0.5, 1.5, (), jnp.float32)
    angle_taps = gaussian(key_of[4], (LAYERS, CHANNELS, ANGLE_TAPS), ANGLE_TAPS ** -0.5, 2.0, (), jnp.float32)
    angle_order = jax.random.permutation(own_keys[5], ANGLES).astype(jnp.int32)
    dilations = draw_dilations(jax.random.fold_in(key_of[7], 71), part)
    return dict(projections=projections, cotangent=cotangent, row_taps=row_taps, channel_mix=channel_mix, angle_taps=angle_taps, angle_order=angle_order, dilations=dilations)


def row_filter(signal, kernel):
    return lax.conv_general_dilated(signal, kernel[:, None, :], (1,), [(ROW_TAPS // 2, ROW_TAPS // 2)], dimension_numbers=('NCH', 'OIH', 'NCH'), feature_group_count=CHANNELS, precision=lax.Precision.HIGHEST)

def rotate(field, offset):
    return jnp.roll(field, -offset, axis=0)

def angular(field, taps, dilation, direction):
    total = jnp.zeros(field.shape, jnp.float32)
    for tap_index in range(ANGLE_TAPS):
        offset = direction * (tap_index - ANGLE_TAPS // 2) * dilation
        total = total + taps[:, tap_index][None, None, :, None] * rotate(field, offset).astype(jnp.float32)
    return total.astype(jnp.bfloat16)

def reference(projections, cotangent, row_taps, channel_mix, angle_taps, angle_order, dilations):
    flat_input = projections.reshape(ANGLES * DET_ROWS, CHANNELS, COLUMNS).astype(jnp.float32)
    rowed_full, pullback = jax.vjp(row_filter, flat_input, row_taps.astype(jnp.float32))
    rowed = rowed_full.astype(jnp.bfloat16)
    mixed = jnp.einsum('ij,njw->niw', channel_mix, rowed.astype(jnp.float32), precision=lax.Precision.HIGHEST).astype(jnp.bfloat16)
    mixed = mixed.reshape(ANGLES, DET_ROWS, CHANNELS, COLUMNS)
    current = jnp.take(mixed, angle_order, axis=0)
    inputs_list = []
    for layer_idx in range(LAYERS):
        inputs_list.append(current)
        current = angular(current, angle_taps[layer_idx], dilations[layer_idx], 1)
    filtered = current
    upstream = cotangent
    grads_list = []
    for layer_idx in reversed(range(LAYERS)):
        layer_input = inputs_list[layer_idx]
        upstream_f = upstream.astype(jnp.float32)
        per_tap = []
        for tap_index in range(ANGLE_TAPS):
            offset = (tap_index - ANGLE_TAPS // 2) * dilations[layer_idx]
            per_tap.append(lax.optimization_barrier(jnp.sum(upstream_f * rotate(layer_input, offset).astype(jnp.float32), axis=(0, 1, 3))))
        grads_list.insert(0, jnp.stack(per_tap, axis=1))
        upstream = angular(upstream, angle_taps[layer_idx], dilations[layer_idx], -1)
    mixed_grad = jnp.zeros(mixed.shape, jnp.bfloat16).at[angle_order].set(upstream)
    mixed_flat = mixed_grad.reshape(ANGLES * DET_ROWS, CHANNELS, COLUMNS).astype(jnp.float32)
    mix_grad = jnp.einsum('niw,njw->ij', mixed_flat, rowed.astype(jnp.float32), precision=lax.Precision.HIGHEST)
    rowed_grad = jnp.einsum('ij,niw->njw', channel_mix, mixed_flat, precision=lax.Precision.HIGHEST).astype(jnp.bfloat16)
    input_grad, row_grad = pullback(rowed_grad.astype(jnp.float32))
    grad_input = input_grad.astype(jnp.bfloat16).reshape(ANGLES, DET_ROWS, CHANNELS, COLUMNS)
    factor = 1.0 / math.sqrt(ANGLES * DET_ROWS * COLUMNS)
    return (filtered, grad_input, row_grad * factor, mix_grad * factor, jnp.stack(grads_list, axis=0) * factor)
```

```python
import functools
import math

import jax
import jax.numpy as jnp
from jax import lax
from jax.experimental import pallas as pl
from jax.experimental.pallas import tpu as pltpu
from jax.sharding import PartitionSpec as P

CHANNELS = 16
COLUMNS = 2048
ROW_TAPS = 65
ANGLE_TAPS = 9
LAYERS = 3
LANES = 128
BLOCK = 256
WINDOW = 512
LEAD = 128
FIRST = LEAD - ROW_TAPS // 2
BF = jnp.bfloat16
F32 = jnp.float32
I32 = jnp.int32
EXACT = lax.Precision.HIGHEST


def iota(shape, dim):
    return lax.broadcasted_iota(I32, shape, dim)


def dot(a, b, ca, cb, precision=None):
    return lax.dot_general(
        a, b, (((ca,), (cb,)), ((), ())), precision=precision, preferred_element_type=F32
    )


def roll(x, shift):
    width = x.shape[-1]
    shift = shift % width
    return x if shift == 0 else pltpu.roll(x, shift, x.ndim - 1)


def toeplitz(row):
    x = jnp.broadcast_to(row, (8, WINDOW))
    at = iota((8, WINDOW), 0)
    for bit in (1, 2, 4):
        x = jnp.where((at & bit) != 0, roll(x, bit), x)
    height = 8
    while height < BLOCK:
        x = jnp.concatenate([x, roll(x, height)], axis=0)
        height *= 2
    return x


def diagonals(x):
    height = x.shape[0] // 2
    while height >= 8:
        x = x[:height] + roll(x[height:], -height)
        height //= 2
    at = iota((8, WINDOW), 0)
    for bit in (4, 2, 1):
        x = jnp.where((at & bit) != 0, roll(x, -bit), x)
    return jnp.sum(x, axis=0, keepdims=True)


def circular(a, b, size, sign):
    total = jnp.zeros_like(b)
    for u in range(size):
        total = total + a[:, u : u + 1] * roll(b, sign * u)
    return total


def kernel(
    n,
    angles,
    scale,
    dil_ref,
    small_ref,
    proj_ref,
    cot_hbm,
    filt_hbm,
    gin_hbm,
    row_out,
    mix_out,
    ang_out,
    x_ref,
    cot_ref,
    xp_ref,
    rgp_ref,
    mid_ref,
    gi_ref,
    mbig_ref,
    mhi_ref,
    mlo_ref,
    thi_ref,
    tlo_ref,
    gram_ref,
    tf_ref,
    tb_ref,
    res_ref,
    gath_ref,
    local_sem,
    xs_sem,
    xr_sem,
    gs_sem,
    gr_sem,
    ws_sem,
    wr_sem,
):
    per = angles // n
    depth = angles * CHANNELS
    bits = angles.bit_length() - 1
    me = lax.axis_index("ang")

    def partner(mask):
        if n & (n - 1):
            return lax.rem(me + mask, n)
        out = 0
        step = 1
        while step < n:
            digit = lax.rem(me // step, 2)
            out = out + step * ((1 - digit) if mask & step else digit)
            step *= 2
        return out

    order = list(range(n - 1, 0, -1))

    cot_copy = pltpu.make_async_copy(cot_hbm.at[:, 0], cot_ref, local_sem.at[0])
    cot_copy.start()
    own_copy = pltpu.make_async_copy(
        proj_ref.at[:, me], x_ref.at[pl.ds(me * per, per)], local_sem.at[1]
    )
    own_copy.start()

    barrier = pltpu.get_barrier_semaphore()
    for mask in order:
        pl.semaphore_signal(
            barrier, inc=1, device_id={"ang": partner(mask)}, device_id_type=pl.DeviceIdType.MESH
        )
    pl.semaphore_wait(barrier, n - 1)

    sends = []
    for mask in order:
        to = partner(mask)
        copy = pltpu.make_async_remote_copy(
            src_ref=proj_ref.at[:, to],
            dst_ref=x_ref.at[pl.ds(me * per, per)],
            send_sem=xs_sem.at[mask],
            recv_sem=xr_sem.at[mask],
            device_id={"ang": to},
            device_id_type=pl.DeviceIdType.MESH,
        )
        copy.start()
        sends.append(copy)

    lane = iota((CHANNELS, LANES), 1)
    spot = lane & (angles - 1)
    row_taps = small_ref[0:CHANNELS, :]
    mix = small_ref[CHANNELS : 2 * CHANNELS, :]
    order_row = small_ref[2 * CHANNELS : 2 * CHANNELS + 1, :]
    tap_from = iota((LANES, WINDOW), 0)
    tap_to = iota((LANES, WINDOW), 1)
    tf_ref[...] = dot(row_taps, (tap_to == FIRST + tap_from).astype(F32), 1, 0, EXACT)
    tb_ref[...] = dot(
        row_taps, (tap_to == FIRST + ROW_TAPS - 1 - tap_from).astype(F32), 1, 0, EXACT
    )

    def taps_of(layer):
        start = (3 + layer) * CHANNELS
        return small_ref[start : start + CHANNELS, :]

    def at_tap(layer, k):
        return (spot == (((k - ANGLE_TAPS // 2) * dil_ref[layer]) & (angles - 1))).astype(F32)

    spread = []
    for layer in range(LAYERS):
        taps = taps_of(layer)
        total = jnp.zeros((CHANNELS, LANES), F32)
        for k in range(ANGLE_TAPS):
            total = total + taps[:, k : k + 1] * at_tap(layer, k)
        spread.append(total)
    whole = circular(spread[2], circular(spread[1], spread[0], angles, 1), angles, 1)
    turned = jnp.concatenate(
        [jnp.where(lane < angles, roll(whole, p), 0.0) for p in range(angles)], axis=0
    )
    wide = iota((depth, LANES), 0)
    wide_lane = iota((depth, LANES), 1)
    select = ((wide & (angles - 1)).astype(F32) == order_row).astype(F32)
    member = ((wide >> bits) == wide_lane).astype(F32)
    mix_row = dot(mix, member, 1, 1, EXACT)
    big = dot(turned, select, 1, 1, EXACT)
    mbig_ref[...] = big
    full = (big.reshape(angles, CHANNELS, depth) * mix_row[None]).reshape(depth, depth)
    high = full.astype(BF)
    mhi_ref[...] = high
    mlo_ref[...] = (full - high.astype(F32)).astype(BF)
    flipped = full.T
    high = flipped.astype(BF)
    thi_ref[...] = high
    tlo_ref[...] = (flipped - high.astype(F32)).astype(BF)

    for ref in (xp_ref, rgp_ref):
        ref[:, :LEAD] = jnp.zeros((depth, LEAD), BF)
        ref[:, LEAD + COLUMNS :] = jnp.zeros((depth, LEAD), BF)

    chunks = COLUMNS // WINDOW

    def columns(i, lead=0):
        return pl.ds(pl.multiple_of(i * WINDOW + lead, LANES), WINDOW)

    blocks = COLUMNS // BLOCK

    def windowed(ref, rows):
        return jnp.concatenate(
            [ref[rows, b * BLOCK : b * BLOCK + WINDOW] for b in range(blocks)], axis=0
        )

    def rows_of(c):
        return pl.ds(pl.multiple_of(c * angles, angles), angles)

    def convolve(ref, taps_ref, c):
        band = toeplitz(taps_ref[pl.ds(c, 1), :]).astype(BF)
        frames = windowed(ref, rows_of(c))
        out = dot(frames, band, 1, 1).astype(BF)
        for b in range(blocks):
            mid_ref[rows_of(c), b * BLOCK : (b + 1) * BLOCK] = out[b * angles : (b + 1) * angles]
        return frames

    cot_copy.wait()

    @pl.loop(0, chunks)
    def _(i):
        part = cot_ref[:, :, columns(i)].reshape(depth, WINDOW)
        out = dot(thi_ref[...], part, 1, 0) + dot(tlo_ref[...], part, 1, 0)
        rgp_ref[:, columns(i, LEAD)] = out.astype(BF)

    @pl.loop(0, CHANNELS)
    def _(c):
        convolve(rgp_ref, tb_ref, c)

    def shuffle(transposed):
        major = iota((depth, depth), 1 if transposed else 0)
        minor = iota((depth, depth), 0 if transposed else 1)
        same_angle = (major & (angles - 1)) == (minor >> 4)
        same_channel = (major >> bits) == (minor & (CHANNELS - 1))
        return jnp.where(same_angle & same_channel, 1.0, 0.0).astype(BF)

    gram_ref[...] = shuffle(True).astype(F32)

    @pl.loop(0, chunks)
    def _(i):
        out = dot(gram_ref[...].astype(BF), mid_ref[:, columns(i)], 1, 0).astype(BF)
        gi_ref[:, :, columns(i)] = out.reshape(angles, CHANNELS, WINDOW)

    for mask in order:
        to = partner(mask)
        copy = pltpu.make_async_remote_copy(
            src_ref=gi_ref.at[pl.ds(to * per, per)],
            dst_ref=gin_hbm.at[:, me],
            send_sem=gs_sem.at[mask],
            recv_sem=gr_sem.at[mask],
            device_id={"ang": to},
            device_id_type=pl.DeviceIdType.MESH,
        )
        copy.start()
        sends.append(copy)
    own_grad = pltpu.make_async_copy(
        gi_ref.at[pl.ds(me * per, per)], gin_hbm.at[:, me], local_sem.at[2]
    )
    own_grad.start()

    own_copy.wait()
    for copy in sends[: n - 1]:
        copy.wait_recv()
    gram_ref[...] = shuffle(False).astype(F32)

    @pl.loop(0, chunks)
    def _(i):
        part = x_ref[:, :, columns(i)].reshape(depth, WINDOW)
        xp_ref[:, columns(i, LEAD)] = dot(gram_ref[...].astype(BF), part, 1, 0).astype(BF)

    @pl.loop(0, CHANNELS)
    def _(c):
        frames = convolve(xp_ref, tf_ref, c)
        grads = jnp.concatenate(
            [
                rgp_ref[rows_of(c), LEAD + b * BLOCK : LEAD + (b + 1) * BLOCK]
                for b in range(blocks)
            ],
            axis=0,
        )
        sums = diagonals(dot(grads, frames, 0, 0))
        res_ref[pl.ds(c, 1), :] = roll(sums, -FIRST)[:, :LANES]

    gram_ref[...] = jnp.zeros((depth, depth), F32)

    @pl.loop(0, chunks)
    def _(i):
        rowed = mid_ref[:, columns(i)]
        out = dot(mhi_ref[...], rowed, 1, 0) + dot(mlo_ref[...], rowed, 1, 0)
        x_ref[:, :, columns(i)] = out.astype(BF).reshape(angles, CHANNELS, WINDOW)
        part = cot_ref[:, :, columns(i)].reshape(depth, WINDOW)
        gram_ref[...] += dot(part, rowed, 1, 1)

    filt_copy = pltpu.make_async_copy(x_ref, filt_hbm.at[:, 0], local_sem.at[3])
    filt_copy.start()

    gram = gram_ref[...]
    weighted = (mbig_ref[...] * gram).reshape(angles, CHANNELS, depth)
    res_ref[CHANNELS : 2 * CHANNELS, :] = dot(jnp.sum(weighted, axis=0), member, 1, 0, EXACT)
    mixed = (gram.reshape(angles, CHANNELS, depth) * mix_row[None]).reshape(depth, depth)
    ranked = dot(mixed, select, 1, 0, EXACT)
    lags = jnp.zeros((CHANNELS, LANES), F32)
    for p in range(angles):
        lags = lags + roll(ranked[p * CHANNELS : (p + 1) * CHANNELS], -p)
    late = circular(spread[2], lags, angles, -1)
    early = circular(spread[0], lags, angles, -1)
    series = [
        circular(spread[1], late, angles, -1),
        circular(spread[0], late, angles, -1),
        circular(spread[1], early, angles, -1),
    ]
    for layer in range(LAYERS):
        once = jnp.where(lane < angles, series[layer], 0.0)
        total = jnp.zeros((CHANNELS, LANES), F32)
        for k in range(ANGLE_TAPS):
            value = jnp.sum(once * at_tap(layer, k), axis=1, keepdims=True)
            total = total + jnp.where(lane == k, value, 0.0)
        res_ref[(2 + layer) * CHANNELS : (3 + layer) * CHANNELS, :] = total

    shares = []
    for mask in order:
        copy = pltpu.make_async_remote_copy(
            src_ref=res_ref,
            dst_ref=gath_ref.at[me],
            send_sem=ws_sem.at[mask],
            recv_sem=wr_sem.at[mask],
            device_id={"ang": partner(mask)},
            device_id_type=pl.DeviceIdType.MESH,
        )
        copy.start()
        shares.append(copy)
    gath_ref[me] = res_ref[...]
    for copy in shares:
        copy.wait_recv()
    total = gath_ref[0]
    for i in range(1, n):
        total = total + gath_ref[i]
    total = total * scale
    row_out[...] = total[:CHANNELS, :ROW_TAPS]
    mix_out[...] = total[CHANNELS : 2 * CHANNELS, :CHANNELS]
    for layer in range(LAYERS):
        start = (2 + layer) * CHANNELS
        ang_out[layer] = total[start : start + CHANNELS, :ANGLE_TAPS]

    filt_copy.wait()
    own_grad.wait()
    for copy in sends[n - 1 :]:
        copy.wait_recv()
    for copy in sends + shares:
        copy.wait_send()


def on_device(n, projections, cotangent, row_taps, channel_mix, angle_taps, angle_order, dilations):
    per, rows = projections.shape[:2]
    angles = per * n
    depth = angles * CHANNELS
    scale = 1.0 / math.sqrt(angles * rows * COLUMNS)

    def wide(x):
        return jnp.pad(x.astype(F32), ((0, 0), (0, LANES - x.shape[1])))

    order_rows = jnp.broadcast_to(
        jnp.tile(angle_order.astype(F32), LANES // angles)[None], (CHANNELS, LANES)
    )
    small = jnp.concatenate(
        [
            wide(row_taps),
            wide(channel_mix),
            order_rows,
            wide(angle_taps.reshape(LAYERS * CHANNELS, ANGLE_TAPS)),
        ],
        axis=0,
    )
    vmem = pl.BlockSpec(memory_space=pltpu.VMEM)
    hbm = pl.BlockSpec(memory_space=pl.ANY)
    padded = COLUMNS + 2 * LEAD
    slots = pltpu.SemaphoreType.DMA((n,))
    field = pltpu.VMEM((angles, CHANNELS, COLUMNS), BF)
    square = pltpu.VMEM((depth, depth), BF)
    exact = pltpu.VMEM((depth, depth), F32)
    results = (2 + LAYERS) * CHANNELS
    return pl.pallas_call(
        functools.partial(kernel, n, angles, scale),
        out_shape=(
            jax.ShapeDtypeStruct(cotangent.shape, BF),
            jax.ShapeDtypeStruct(projections.shape, BF),
            jax.ShapeDtypeStruct((CHANNELS, ROW_TAPS), F32),
            jax.ShapeDtypeStruct((CHANNELS, CHANNELS), F32),
            jax.ShapeDtypeStruct((LAYERS, CHANNELS, ANGLE_TAPS), F32),
        ),
        in_specs=[pl.BlockSpec(memory_space=pltpu.SMEM), vmem, hbm, hbm],
        out_specs=(hbm, hbm, vmem, vmem, vmem),
        scratch_shapes=[
            field,
            field,
            pltpu.VMEM((depth, padded), BF),
            pltpu.VMEM((depth, padded), BF),
            pltpu.VMEM((depth, COLUMNS), BF),
            field,
            exact,
            square,
            square,
            square,
            square,
            exact,
            pltpu.VMEM((CHANNELS, WINDOW), F32),
            pltpu.VMEM((CHANNELS, WINDOW), F32),
            pltpu.VMEM((results, LANES), F32),
            pltpu.VMEM((n, results, LANES), F32),
            pltpu.SemaphoreType.DMA((4,)),
            slots,
            slots,
            slots,
            slots,
            slots,
            slots,
        ],
        compiler_params=pltpu.CompilerParams(
            collective_id=0, has_side_effects=True, vmem_limit_bytes=60 * 1024 * 1024
        ),
    )(dilations, small, projections, cotangent)


def solution(mesh):
    return jax.shard_map(
        functools.partial(on_device, mesh.shape["ang"]),
        mesh=mesh,
        in_specs=(
            P(("grp", "ang"), None, None, None),
            P("grp", "ang", None, None),
            P(),
            P(),
            P(),
            P("grp"),
            P(),
        ),
        out_specs=(
            P("grp", "ang", None, None),
            P(("grp", "ang"), None, None, None),
            P("grp", None),
            P("grp", None),
            P("grp", None, None),
        ),
        check_vma=False,
    )
```
